32 devices in a mesh: patch: 2 (over x), col: 16 (over z, y, core).
Axes of the slice: x: 2, y: 2, z: 4, core: 2. Of those that a mesh axis runs over, the one named last changes fastest.
Arguments:
- sources_field: bfloat16 [8, 2048, 256], P('patch', 'col'), parts along dimension 0, may hold values from -6 to 6
- residual_field: bfloat16 [8, 2048, 256], P('patch', 'col'), parts along dimension 0, may hold values from -6 to 6
- v_factors: bfloat16 [8, 2, 2048, 384], P('patch', None, 'col'), parts along dimension 0, may hold values from -0.25 to 0.25
- u_factors: bfloat16 [8, 2, 2048, 384], P('patch', None, 'col'), parts along dimension 0, may hold values from -0.375 to 0.375
- tile_class: int32 [8, 8, 8], P('patch'), parts along dimension 0, may hold values from 0 to 3, as said below
Outputs:
- forward_field: bfloat16 [8, 2048, 256], P('patch', 'col'), parts along dimension 0
- adjoint_field: bfloat16 [8, 2048, 256], P('patch', 'col'), parts along dimension 0
The draws below stay inside these ranges and needn't reach their ends.
There are 2 independent parts, one for each index of `patch`. The reference program is written for one: setup_inputs(seed, part) draws one part's arguments, and reference() takes and returns one part's arrays. A program takes and returns all parts, laid end to end along the dimension named above; each array names one. Nothing has to cross between parts.
Inputs may be any that keep to these rules, and one draw needn't show every extreme that they name: `tile_class`: in every frequency, every tile row and every tile column holds exactly 2 tiles of class 0, 3 of class 1, 2 of class 2 and 1 of class 3.
All inputs are finite; a program needn't handle non-finite values.
Results may differ from the reference program's by a relative error of at most 0.0058.
Values may be sent and summed in bfloat16 or wider, within the bound.
A program may use at most 128 MiB of HBM per device.

```python
import jax
import jax.numpy as jnp
from jax import lax

TILE = 256
FREQS = 4
POINTS = 128
RANK0 = 8
RANK1 = 16
RANK2 = 32
RANK3 = 48
HALF = 128
TILES = 8
SOURCES = 2048
RECEIVERS = 2048


def draw_tile_class(key, part):
    key = jax.random.fold_in(key, 17)
    freq_keys = jax.random.split(key, FREQS)

    def one_frequency(freq_key):
        key_base, key_row, key_col = jax.random.split(freq_key, 3)
        positions = jnp.arange(TILES, dtype=jnp.int32)
        first_edge = TILES // 4
        second_edge = first_edge + 3 * TILES // 8
        third_edge = TILES - TILES // 8
        base_classes = (positions >= first_edge).astype(jnp.int32) + (positions >= second_edge).astype(jnp.int32) + (positions >= third_edge).astype(jnp.int32)
        base_classes = jax.random.permutation(key_base, base_classes).astype(jnp.int32)
        row_shift = jax.random.permutation(key_row, TILES).astype(jnp.int32)
        col_shift = jax.random.permutation(key_col, TILES).astype(jnp.int32)
        return base_classes[(row_shift[:, None] + col_shift[None, :]) % TILES]
    return jax.vmap(one_frequency)(freq_keys).astype(jnp.int32)


def shard_levels(rng, extent, cuts, least, high):
    def one(dim, parts):
        steps = jax.random.uniform(jax.random.fold_in(jax.random.fold_in(rng, 6), dim), (parts,), jnp.float32, least / len(cuts), high / len(cuts))
        return jnp.repeat(jnp.exp(steps), extent[dim] // parts).reshape((-1,) + (1,) * (len(extent) - dim - 1))

    gain = one(*cuts[0])
    for cut in cuts[1:]:
        gain = gain * one(*cut)
    return gain


def normal_values(key, dims, scale, bound, cuts=(), kind=jnp.bfloat16):
    loudness = shard_levels(key, dims, cuts, -0.22, 0.18) if cuts else 1.0
    array = jax.random.normal(key, dims, jnp.float32) * scale * loudness
    return jnp.minimum(jnp.maximum(array, -bound), bound).astype(kind)


def setup_inputs(seed: int = 0, part: int = 0) -> dict:
    key_of = jax.random.split(jax.random.key(seed), 6)
    own_keys = jax.random.split(jax.random.fold_in(key_of[5], part), 6)
    return {
        "sources_field": normal_values(own_keys[0], (FREQS, SOURCES, 2 * POINTS), 1.0, 6.0, ((1, 16),)),
        "residual_field": normal_values(own_keys[1], (FREQS, RECEIVERS, 2 * POINTS), 1.0, 6.0, ((1, 16),)),
        "v_factors": normal_values(own_keys[2], (FREQS, 2, SOURCES, TILES * RANK3), (2 * TILE) ** -0.5, 0.25, ((2, 16),)),
        "u_factors": normal_values(own_keys[3], (FREQS, 2, RECEIVERS, TILES * RANK3), (2 * TILES * RANK1) ** -0.5, 0.375, ((2, 16),)),
        "tile_class": draw_tile_class(jax.random.fold_in(jax.random.fold_in(key_of[5], part), 71), part),
    }


def class_widths(classes):
    return ((classes == 0).astype(jnp.int32) * RANK0 + (classes == 1).astype(jnp.int32) * RANK1
            + (classes == 2).astype(jnp.int32) * RANK2 + (classes == 3).astype(jnp.int32) * RANK3)


def contract(matrix, vector):
    return jnp.einsum('bhrok,bhrp->obhkp', matrix, vector)


def expand(matrix, vector):
    return jnp.einsum('orbk,obkp->orp', matrix, vector)


def apply_kernel(source_factor, field_block, target_factor, tile_widths):
    source_f32 = source_factor.astype(jnp.float32).reshape(2, TILES, 2, HALF, TILES, RANK3)
    field_f32 = field_block.astype(jnp.float32).reshape(TILES, 2, HALF, 2, POINTS)
    factor_re, factor_im = source_f32[0], source_f32[1]
    field_re, field_im = field_f32[:, :, :, 0], field_f32[:, :, :, 1]
    real_sum = contract(factor_re, field_re) + contract(factor_im, field_im)
    imag_sum = contract(factor_re, field_im) - contract(factor_im, field_re)
    partial_value = jnp.stack([real_sum, imag_sum], axis=4)
    alive_mask = jnp.arange(RANK3, dtype=jnp.int32)[None, None, :] < tile_widths[:, :, None]
    partial_value = jnp.where(alive_mask[:, :, None, :, None, None], partial_value, 0.0)
    partial_value = lax.optimization_barrier(partial_value.astype(jnp.bfloat16)).astype(jnp.float32)
    summed = partial_value[:, :, 0] + partial_value[:, :, 1]
    summed = lax.optimization_barrier(summed.astype(jnp.bfloat16)).astype(jnp.float32)
    target_f32 = target_factor.astype(jnp.float32).reshape(2, TILES, TILE, TILES, RANK3)
    coeff_re, coeff_im = summed[:, :, :, 0], summed[:, :, :, 1]
    out_real = expand(target_f32[0], coeff_re) - expand(target_f32[1], coeff_im)
    out_imag = expand(target_f32[0], coeff_im) + expand(target_f32[1], coeff_re)
    joined = jnp.concatenate([out_real, out_imag], axis=-1)
    return joined.reshape(TILES * TILE, 2 * POINTS).astype(jnp.bfloat16)


def reference(sources_field, residual_field, v_factors, u_factors, tile_class):
    def per_frequency(sliced):
        source_slice, residual_slice, v_slice, u_slice, class_slice = sliced
        widths = class_widths(class_slice)
        forward = apply_kernel(v_slice, source_slice, u_slice, widths)
        adjoint = apply_kernel(u_slice, residual_slice, v_slice, widths.T)
        return forward, adjoint

    forward_field, adjoint_field = lax.map(
        per_frequency, (sources_field, residual_field, v_factors, u_factors, tile_class))
    return (forward_field, adjoint_field)
```

```python
import jax
import jax.numpy as jnp
from jax import lax
from jax.experimental import pallas as pl
from jax.experimental.pallas import tpu as pltpu
from jax.sharding import PartitionSpec as P

RANKS = (8, 16, 32, 48)
CORES = 2
GROUP = 384
VMEM_LIMIT = 56 * 1024 * 1024


def flipped(index, step, count):
    if count & (count - 1):
        return (index + step) % count
    out = index
    bit = 1
    while bit < count:
        if step & bit:
            out = out + (1 - 2 * ((index // bit) % 2)) * bit
        bit *= 2
    return out


def partner_steps(count):
    steps = []
    top = count // 2
    while top >= 1:
        steps += list(range(top, min(2 * top, count)))
        top //= 2
    return steps if not count & (count - 1) else list(range(1, count))


def kernel(
    class_ref, x_ref, r_ref, v_ref, u_ref, fwd_ref, adj_ref,
    v_all, u_all, x_all, r_all, coeff, got, result,
    in_sem, in_send, in_recv, send_sem, recv_sem, out_sem, out_send, out_recv,
):
    freqs, _, half_rows, width = v_ref.shape
    tiles = class_ref.shape[1]
    rank = width // tiles
    points = x_ref.shape[2] // 2
    own = freqs // CORES
    index = lax.axis_index("col")
    tile = index // CORES
    side = index % CORES
    sibling = tile * CORES + 1 - side
    first = side * own
    other_first = (1 - side) * own
    steps = partner_steps(tiles)

    loads = ((v_ref, v_all), (x_ref, x_all), (u_ref, u_all), (r_ref, r_all))

    def local_load(a, f):
        src, dst = loads[a]
        return pltpu.make_async_copy(src.at[first + f], dst.at[f, side], in_sem.at[a, f])

    def remote_load(a, f):
        src, dst = loads[a]
        return pltpu.make_async_remote_copy(
            src_ref=src.at[other_first + f], dst_ref=dst.at[f, side],
            send_sem=in_send.at[a, f], recv_sem=in_recv.at[a, f],
            device_id={"col": sibling}, device_id_type=pl.DeviceIdType.MESH,
        )

    pairs = [(d, f) for d in range(2) for f in range(own)]
    for d, f in pairs:
        local_load(2 * d, f).start()
        local_load(2 * d + 1, f).start()

    barrier = pltpu.get_barrier_semaphore()
    pl.semaphore_signal(barrier, inc=1, device_id={"col": sibling}, device_id_type=pl.DeviceIdType.MESH)
    for step in steps:
        peer = flipped(tile, step, tiles) * CORES + side
        pl.semaphore_signal(barrier, inc=1, device_id={"col": peer}, device_id_type=pl.DeviceIdType.MESH)
    pl.semaphore_wait(barrier, tiles)

    for d, f in pairs:
        remote_load(2 * d, f).start()
        remote_load(2 * d + 1, f).start()

    def send(d, f, step):
        peer = flipped(tile, step, tiles)
        return pltpu.make_async_remote_copy(
            src_ref=coeff.at[d, f, peer], dst_ref=got.at[d, f, tile],
            send_sem=send_sem.at[d, f, step], recv_sem=recv_sem.at[d, f, step],
            device_id={"col": peer * CORES + side}, device_id_type=pl.DeviceIdType.MESH,
        )

    row = lax.broadcasted_iota(jnp.int32, (rank, 2 * points), 0)
    for d, f in pairs:
        factor, field = ((v_all, x_all), (u_all, r_all))[d]
        for a in (2 * d, 2 * d + 1):
            local_load(a, f).wait()
            remote_load(a, f).wait_recv()
        parts = []
        for half in range(CORES):
            block = field[f, half]
            parts += [block, jnp.concatenate([block[:, points:], -block[:, :points]], axis=1)]
        operand = jnp.concatenate(parts, axis=0)
        group = GROUP if width % GROUP == 0 else width
        for g in range(width // group):
            stacked = factor[f, :, :, :, g * group:(g + 1) * group]
            stacked = stacked.reshape(2 * CORES * half_rows, group)
            sums = lax.dot_general(
                stacked, operand, (((0,), (0,)), ((), ())), preferred_element_type=jnp.float32)
            for k in range(group // rank):
                to = g * (group // rank) + k
                cls = class_ref[first + f, to, tile] if d == 0 else class_ref[first + f, tile, to]
                alive = jnp.where(cls == 0, RANKS[0], jnp.where(
                    cls == 1, RANKS[1], jnp.where(cls == 2, RANKS[2], RANKS[3])))
                kept = jnp.where(row < alive, sums[k * rank:(k + 1) * rank], 0.0)
                coeff[d, f, to] = kept.astype(jnp.bfloat16)
        for step in steps:
            send(d, f, step).start()

    def outputs(d, f):
        out = (fwd_ref, adj_ref)[d]
        local = pltpu.make_async_copy(result.at[d, f, side], out.at[first + f], out_sem.at[d, f])
        remote = pltpu.make_async_remote_copy(
            src_ref=result.at[d, f, 1 - side], dst_ref=out.at[first + f],
            send_sem=out_send.at[d, f], recv_sem=out_recv.at[d, f],
            device_id={"col": sibling}, device_id_type=pl.DeviceIdType.MESH,
        )
        return local, remote

    for d, f in pairs:
        factor = (u_all, v_all)[d]
        got[d, f, tile] = coeff[d, f, tile]
        for step in steps:
            send(d, f, step).wait_recv()
        values = got[d, f].reshape(width, 2 * points)
        turned = jnp.concatenate([-values[:, points:], values[:, :points]], axis=1)
        real_rows = factor[f, :, 0].reshape(CORES * half_rows, width)
        imag_rows = factor[f, :, 1].reshape(CORES * half_rows, width)
        total = jnp.dot(real_rows, values, preferred_element_type=jnp.float32)
        total = total + jnp.dot(imag_rows, turned, preferred_element_type=jnp.float32)
        result[d, f] = total.astype(jnp.bfloat16).reshape(CORES, half_rows, 2 * points)
        local, remote = outputs(d, f)
        remote.start()
        local.start()

    for d, f in pairs:
        for a in (2 * d, 2 * d + 1):
            remote_load(a, f).wait_send()
        for step in steps:
            send(d, f, step).wait_send()
        local, remote = outputs(d, f)
        local.wait()
        remote.wait()


def body(sources_field, residual_field, v_factors, u_factors, tile_class):
    freqs, _, half_rows, width = v_factors.shape
    tiles = tile_class.shape[1]
    points2 = sources_field.shape[2]
    own = freqs // CORES
    steps = max(tiles, 2)
    any_spec = pl.BlockSpec(memory_space=pl.ANY)
    dma = pltpu.SemaphoreType.DMA
    bf16 = jnp.bfloat16
    out = jax.ShapeDtypeStruct(sources_field.shape, bf16)
    flops = 2 * 2 * 2 * freqs * 2 * half_rows * width * points2
    return pl.pallas_call(
        kernel,
        out_shape=(out, out),
        in_specs=[pl.BlockSpec(memory_space=pltpu.SMEM)] + [any_spec] * 4,
        out_specs=(any_spec, any_spec),
        scratch_shapes=[
            pltpu.VMEM((own, CORES, 2, half_rows, width), bf16),
            pltpu.VMEM((own, CORES, 2, half_rows, width), bf16),
            pltpu.VMEM((own, CORES, half_rows, points2), bf16),
            pltpu.VMEM((own, CORES, half_rows, points2), bf16),
            pltpu.VMEM((2, own, tiles, width // tiles, points2), bf16),
            pltpu.VMEM((2, own, tiles, width // tiles, points2), bf16),
            pltpu.VMEM((2, own, CORES, half_rows, points2), bf16),
            dma((4, own)), dma((4, own)), dma((4, own)),
            dma((2, own, steps)), dma((2, own, steps)),
            dma((2, own)), dma((2, own)), dma((2, own)),
        ],
        compiler_params=pltpu.CompilerParams(
            collective_id=0, has_side_effects=True, vmem_limit_bytes=VMEM_LIMIT),
        cost_estimate=pl.CostEstimate(
            flops=flops, transcendentals=0, bytes_accessed=4 * v_factors.size + 8 * sources_field.size),
    )(tile_class, sources_field, residual_field, v_factors, u_factors)


def solution(mesh):
    placed = (
        P("patch", "col", None),
        P("patch", "col", None),
        P("patch", None, "col", None),
        P("patch", None, "col", None),
        P("patch", None, None),
    )
    return jax.shard_map(
        body,
        mesh=mesh,
        in_specs=placed,
        out_specs=(P("patch", "col", None), P("patch", "col", None)),
        check_vma=False,
    )
```

```python
import jax
import jax.numpy as jnp
from jax import lax
from jax.experimental import pallas as pl
from jax.experimental.pallas import tpu as pltpu
from jax.sharding import PartitionSpec as P

RANKS = (8, 16, 32, 48)
CORES = 2
GROUP = 384
VMEM_LIMIT = 56 * 1024 * 1024


def flipped(index, step, count):
    if count & (count - 1):
        return (index + step) % count
    out = index
    bit = 1
    while bit < count:
        if step & bit:
            out = out + (1 - 2 * ((index // bit) % 2)) * bit
        bit *= 2
    return out


def partner_steps(count):
    steps = []
    top = count // 2
    while top >= 1:
        steps += list(range(top, min(2 * top, count)))
        top //= 2
    return steps if not count & (count - 1) else list(range(1, count))


def kernel(
    class_ref, x_ref, r_ref, v_ref, u_ref, fwd_ref, adj_ref,
    v_all, u_all, x_all, r_all, coeff, got, result,
    in_sem, in_send, in_recv, send_sem, recv_sem, out_send, out_recv,
):
    freqs, _, half_rows, width = v_ref.shape
    tiles = class_ref.shape[1]
    rank = width // tiles
    points = x_ref.shape[2] // 2
    own = freqs // CORES
    index = lax.axis_index("col")
    tile = index // CORES
    side = index % CORES
    sibling = tile * CORES + 1 - side
    first = side * own
    other_first = (1 - side) * own
    steps = partner_steps(tiles)

    loads = ((v_ref, v_all), (x_ref, x_all), (u_ref, u_all), (r_ref, r_all))

    def local_load(a, f):
        src, dst = loads[a]
        return pltpu.make_async_copy(src.at[first + f], dst.at[f, side], in_sem.at[a, f])

    def remote_load(a, f):
        src, dst = loads[a]
        return pltpu.make_async_remote_copy(
            src_ref=src.at[other_first + f], dst_ref=dst.at[f, side],
            send_sem=in_send.at[a, f], recv_sem=in_recv.at[a, f],
            device_id={"col": sibling}, device_id_type=pl.DeviceIdType.MESH,
        )

    pairs = [(d, f) for d in range(2) for f in range(own)]
    for d, f in pairs:
        local_load(2 * d, f).start()
        local_load(2 * d + 1, f).start()

    barrier = pltpu.get_barrier_semaphore()
    pl.semaphore_signal(barrier, inc=1, device_id={"col": sibling}, device_id_type=pl.DeviceIdType.MESH)
    for step in steps:
        peer = flipped(tile, step, tiles) * CORES + side
        pl.semaphore_signal(barrier, inc=1, device_id={"col": peer}, device_id_type=pl.DeviceIdType.MESH)
    pl.semaphore_wait(barrier, tiles)

    for d, f in pairs:
        remote_load(2 * d, f).start()
        remote_load(2 * d + 1, f).start()

    def send(d, f, step):
        peer = flipped(tile, step, tiles)
        return pltpu.make_async_remote_copy(
            src_ref=coeff.at[d, f, peer], dst_ref=got.at[d, f, tile],
            send_sem=send_sem.at[d, f, step], recv_sem=recv_sem.at[d, f, step],
            device_id={"col": peer * CORES + side}, device_id_type=pl.DeviceIdType.MESH,
        )

    row = lax.broadcasted_iota(jnp.int32, (rank, 2 * points), 0)
    for d, f in pairs:
        factor, field = ((v_all, x_all), (u_all, r_all))[d]
        for a in (2 * d, 2 * d + 1):
            local_load(a, f).wait()
            remote_load(a, f).wait_recv()
        parts = []
        for half in range(CORES):
            block = field[f, half]
            parts += [block, jnp.concatenate([block[:, points:], -block[:, :points]], axis=1)]
        operand = jnp.concatenate(parts, axis=0)
        group = GROUP if width % GROUP == 0 else width
        for g in range(width // group):
            stacked = factor[f, :, :, :, g * group:(g + 1) * group]
            stacked = stacked.reshape(2 * CORES * half_rows, group)
            sums = lax.dot_general(
                stacked, operand, (((0,), (0,)), ((), ())), preferred_element_type=jnp.float32)
            for k in range(group // rank):
                to = g * (group // rank) + k
                cls = class_ref[first + f, to, tile] if d == 0 else class_ref[first + f, tile, to]
                alive = jnp.where(cls == 0, RANKS[0], jnp.where(
                    cls == 1, RANKS[1], jnp.where(cls == 2, RANKS[2], RANKS[3])))
                kept = jnp.where(row < alive, sums[k * rank:(k + 1) * rank], 0.0)
                coeff[d, f, to] = kept.astype(jnp.bfloat16)
        for step in steps:
            send(d, f, step).start()

    def output(d, f):
        return pltpu.make_async_remote_copy(
            src_ref=result.at[d, f, 1 - side], dst_ref=(fwd_ref, adj_ref)[d].at[first + f],
            send_sem=out_send.at[d, f], recv_sem=out_recv.at[d, f],
            device_id={"col": sibling}, device_id_type=pl.DeviceIdType.MESH,
        )

    for d, f in pairs:
        factor = (u_all, v_all)[d]
        got[d, f, tile] = coeff[d, f, tile]
        for step in steps:
            send(d, f, step).wait_recv()
        values = got[d, f].reshape(width, 2 * points)
        turned = jnp.concatenate([-values[:, points:], values[:, :points]], axis=1)
        real_rows = factor[f, :, 0].reshape(CORES * half_rows, width)
        imag_rows = factor[f, :, 1].reshape(CORES * half_rows, width)
        total = jnp.dot(real_rows, values, preferred_element_type=jnp.float32)
        total = total + jnp.dot(imag_rows, turned, preferred_element_type=jnp.float32)
        result[d, f] = total.astype(jnp.bfloat16).reshape(CORES, half_rows, 2 * points)
        output(d, f).start()
        (fwd_ref, adj_ref)[d][first + f] = result[d, f, side]

    for d, f in pairs:
        for a in (2 * d, 2 * d + 1):
            remote_load(a, f).wait_send()
        for step in steps:
            send(d, f, step).wait_send()
        output(d, f).wait()


def copy_out(*refs):
    srcs, dsts, sem = refs[:2], refs[2:4], refs[4]
    copies = [
        pltpu.make_async_copy(src.at[f], dst.at[f], sem.at[n, f])
        for n, (src, dst) in enumerate(zip(srcs, dsts)) for f in range(src.shape[0])
    ]
    for copy in copies:
        copy.start()
    for copy in copies:
        copy.wait()


def body(sources_field, residual_field, v_factors, u_factors, tile_class):
    freqs, _, half_rows, width = v_factors.shape
    tiles = tile_class.shape[1]
    points2 = sources_field.shape[2]
    own = freqs // CORES
    steps = max(tiles, 2)
    any_spec = pl.BlockSpec(memory_space=pl.ANY)
    dma = pltpu.SemaphoreType.DMA
    bf16 = jnp.bfloat16
    out = jax.ShapeDtypeStruct(sources_field.shape, bf16)
    flops = 2 * 2 * 2 * freqs * 2 * half_rows * width * points2
    fields = pl.pallas_call(
        kernel,
        out_shape=(pltpu.VMEM(out.shape, bf16), pltpu.VMEM(out.shape, bf16)),
        in_specs=[pl.BlockSpec(memory_space=pltpu.SMEM)] + [pl.BlockSpec(memory_space=pltpu.HBM)] * 4,
        out_specs=(pl.BlockSpec(memory_space=pltpu.VMEM),) * 2,
        scratch_shapes=[
            pltpu.VMEM((own, CORES, 2, half_rows, width), bf16),
            pltpu.VMEM((own, CORES, 2, half_rows, width), bf16),
            pltpu.VMEM((own, CORES, half_rows, points2), bf16),
            pltpu.VMEM((own, CORES, half_rows, points2), bf16),
            pltpu.VMEM((2, own, tiles, width // tiles, points2), bf16),
            pltpu.VMEM((2, own, tiles, width // tiles, points2), bf16),
            pltpu.VMEM((2, own, CORES, half_rows, points2), bf16),
            dma((4, own)), dma((4, own)), dma((4, own)),
            dma((2, own, steps)), dma((2, own, steps)),
            dma((2, own)), dma((2, own)),
        ],
        compiler_params=pltpu.CompilerParams(
            collective_id=0, has_side_effects=True, vmem_limit_bytes=VMEM_LIMIT),
        cost_estimate=pl.CostEstimate(
            flops=flops, transcendentals=0, bytes_accessed=4 * v_factors.size + 8 * sources_field.size),
    )(tile_class, sources_field, residual_field, v_factors, u_factors)
    return pl.pallas_call(
        copy_out,
        out_shape=(out, out),
        in_specs=[pl.BlockSpec(memory_space=pltpu.VMEM)] * 2,
        out_specs=(any_spec, any_spec),
        scratch_shapes=[dma((2, freqs))],
        compiler_params=pltpu.CompilerParams(vmem_limit_bytes=4 * 1024 * 1024),
    )(*fields)


def solution(mesh):
    placed = (
        P("patch", "col", None),
        P("patch", "col", None),
        P("patch", None, "col", None),
        P("patch", None, "col", None),
        P("patch", None, None),
    )
    return jax.shard_map(
        body,
        mesh=mesh,
        in_specs=placed,
        out_specs=(P("patch", "col", None), P("patch", "col", None)),
        check_vma=False,
    )
```

```python
import jax
import jax.numpy as jnp
from jax import lax
from jax.experimental import pallas as pl
from jax.experimental.pallas import tpu as pltpu
from jax.sharding import PartitionSpec as P

RANKS = (8, 16, 32, 48)
CORES = 2
GROUP = 384
VMEM_LIMIT = 56 * 1024 * 1024
MESH = pl.DeviceIdType.MESH
THROUGH = 2


def packed_rows(tiles):
    return tiles // 8 * RANKS[3] + tiles // 4 * RANKS[2] + tiles // 8 * RANKS[1]


def kernel(
    class_ref, x_ref, r_ref, v_ref, u_ref, fwd_ref, adj_ref,
    v_all, u_all, x_all, r_all, coeff, packed, landed, relayed, got, result,
    in_sem, in_send, in_recv, near_send, far_send, got_recv, pack_send, pack_recv, relay_send,
    out_send, out_recv,
):
    freqs, _, half_rows, width = v_ref.shape
    tiles = class_ref.shape[1]
    rank = width // tiles
    points = x_ref.shape[2] // 2
    own = freqs // CORES
    index = lax.axis_index("col")
    tile = index // CORES
    side = index % CORES
    sibling = tile * CORES + 1 - side
    first = side * own
    other_first = (1 - side) * own
    group = tiles // 2
    inner = tiles // 4
    upper = tile // group
    place = tile % group
    near_base = upper * group
    far_base = (1 - upper) * group
    lane = place % inner
    gate = far_base + lane + upper * (group - inner)
    slot_out = place // inner
    is_gate = (place // inner) == (1 - upper)

    loads = ((v_ref, v_all), (x_ref, x_all), (u_ref, u_all), (r_ref, r_all))

    def local_load(a, f):
        src, dst = loads[a]
        return pltpu.make_async_copy(src.at[first + f], dst.at[f, side], in_sem.at[a, f])

    def remote_load(a, f):
        src, dst = loads[a]
        return pltpu.make_async_remote_copy(
            src_ref=src.at[other_first + f], dst_ref=dst.at[f, side],
            send_sem=in_send.at[a, f], recv_sem=in_recv.at[a, f],
            device_id={"col": sibling}, device_id_type=MESH,
        )

    pairs = [(d, f) for d in range(2) for f in range(own)]
    through = pairs[:THROUGH]
    for d, f in pairs:
        local_load(2 * d, f).start()
        local_load(2 * d + 1, f).start()

    barrier = pltpu.get_barrier_semaphore()
    pl.semaphore_signal(barrier, inc=1, device_id={"col": sibling}, device_id_type=MESH)
    for step in range(1, tiles):
        peer = ((tile + step) % tiles) * CORES + side
        pl.semaphore_signal(barrier, inc=1, device_id={"col": peer}, device_id_type=MESH)
    pl.semaphore_wait(barrier, tiles)

    for d, f in pairs:
        remote_load(2 * d, f).start()
        remote_load(2 * d + 1, f).start()

    def live(d, f, source, target):
        cls = class_ref[first + f, target, source] if d == 0 else class_ref[first + f, source, target]
        return jnp.where(cls == 0, RANKS[0], jnp.where(
            cls == 1, RANKS[1], jnp.where(cls == 2, RANKS[2], RANKS[3])))

    pack_rows = packed.shape[2]

    def selection(d, f, source, base):
        col = lax.broadcasted_iota(jnp.int32, (1, group * rank), 1)
        spot = jnp.full((1, group * rank), -1, jnp.int32)
        start = jnp.int32(0)
        for q in range(group):
            alive = live(d, f, source, base + q)
            inside = (col >= q * rank) & (col < q * rank + alive)
            spot = jnp.where(inside, col + (start - q * rank), spot)
            start = start + alive
        rows = lax.broadcasted_iota(jnp.int32, (pack_rows, group * rank), 0)
        return jnp.where(rows == spot, 1.0, 0.0).astype(jnp.bfloat16)

    def pack_copy(d, f):
        return pltpu.make_async_remote_copy(
            src_ref=packed.at[d, f], dst_ref=landed.at[d, f, slot_out],
            send_sem=pack_send.at[d, f], recv_sem=pack_recv.at[d, f, slot_out],
            device_id={"col": gate * CORES + side}, device_id_type=MESH)

    def pack_wait(d, f, slot):
        return pltpu.make_async_remote_copy(
            src_ref=packed.at[d, f], dst_ref=landed.at[d, f, slot],
            send_sem=pack_send.at[d, f], recv_sem=pack_recv.at[d, f, slot],
            device_id={"col": gate * CORES + side}, device_id_type=MESH)

    def near_copy(d, f, step):
        q = (place + step) % group
        return pltpu.make_async_remote_copy(
            src_ref=coeff.at[d, f, near_base + q], dst_ref=got.at[d, f, tile],
            send_sem=near_send.at[d, f, step], recv_sem=got_recv.at[d, f, tile],
            device_id={"col": (near_base + q) * CORES + side}, device_id_type=MESH)

    def relay_copy(d, f, slot, step):
        q = (place + step) % group
        source = far_base + slot * inner + lane
        return pltpu.make_async_remote_copy(
            src_ref=relayed.at[d, f, slot, q], dst_ref=got.at[d, f, source],
            send_sem=relay_send.at[d, f, slot, step], recv_sem=got_recv.at[d, f, source],
            device_id={"col": (near_base + q) * CORES + side}, device_id_type=MESH)

    def got_wait(d, f, source):
        pltpu.make_async_remote_copy(
            src_ref=coeff.at[d, f, source], dst_ref=got.at[d, f, source],
            send_sem=near_send.at[d, f, 0], recv_sem=got_recv.at[d, f, source],
            device_id={"col": sibling}, device_id_type=MESH).wait_recv()

    def far_copy(d, f, step):
        q = (place + step) % group
        return pltpu.make_async_remote_copy(
            src_ref=coeff.at[d, f, far_base + q], dst_ref=got.at[d, f, tile],
            send_sem=far_send.at[d, f, step], recv_sem=got_recv.at[d, f, tile],
            device_id={"col": (far_base + q) * CORES + side}, device_id_type=MESH)

    row = lax.broadcasted_iota(jnp.int32, (rank, 2 * points), 0)
    for d, f in pairs:
        factor, field = ((v_all, x_all), (u_all, r_all))[d]
        for a in (2 * d, 2 * d + 1):
            local_load(a, f).wait()
            remote_load(a, f).wait_recv()
        parts = []
        for half in range(CORES):
            block = field[f, half]
            parts += [block, jnp.concatenate([block[:, points:], -block[:, :points]], axis=1)]
        operand = jnp.concatenate(parts, axis=0)
        wide = GROUP if width % GROUP == 0 else width
        for g in range(width // wide):
            stacked = factor[f, :, :, :, g * wide:(g + 1) * wide]
            stacked = stacked.reshape(2 * CORES * half_rows, wide)
            sums = lax.dot_general(
                stacked, operand, (((0,), (0,)), ((), ())), preferred_element_type=jnp.float32)
            for k in range(wide // rank):
                to = g * (wide // rank) + k
                alive = live(d, f, tile, to)
                kept = jnp.where(row < alive, sums[k * rank:(k + 1) * rank], 0.0)
                coeff[d, f, to] = kept.astype(jnp.bfloat16)
        for step in range(1, group):
            near_copy(d, f, step).start()
        if (d, f) in through:
            far = coeff[d, f, pl.ds(far_base, group)].reshape(group * rank, 2 * points)
            packed[d, f] = jnp.dot(
                selection(d, f, tile, far_base), far,
                preferred_element_type=jnp.float32).astype(jnp.bfloat16)
            pack_copy(d, f).start()
        else:
            for step in range(group):
                far_copy(d, f, step).start()

    def relay(d, f):
        @pl.when(is_gate)
        def _():
            for slot in range(CORES):
                source = far_base + slot * inner + lane
                pack_wait(d, f, slot).wait_recv()
                full = lax.dot_general(
                    selection(d, f, source, near_base), landed[d, f, slot],
                    (((0,), (0,)), ((), ())), preferred_element_type=jnp.float32)
                relayed[d, f, slot] = full.astype(jnp.bfloat16).reshape(group, rank, 2 * points)
                for step in range(1, group):
                    relay_copy(d, f, slot, step).start()
                got[d, f, source] = relayed[d, f, slot, place]

    def output(d, f):
        return pltpu.make_async_remote_copy(
            src_ref=result.at[d, f, 1 - side], dst_ref=(fwd_ref, adj_ref)[d].at[first + f],
            send_sem=out_send.at[d, f], recv_sem=out_recv.at[d, f],
            device_id={"col": sibling}, device_id_type=MESH,
        )

    for d, f in through:
        relay(d, f)

    for d, f in pairs:
        factor = (u_all, v_all)[d]
        got[d, f, tile] = coeff[d, f, tile]
        for step in range(1, group):
            got_wait(d, f, near_base + (place + step) % group)
        for slot in range(CORES):
            for at in range(inner):
                source = far_base + slot * inner + at
                if (d, f) not in through:
                    got_wait(d, f, source)
                    continue

                @pl.when(jnp.logical_not(is_gate & (lane == at)))
                def _():
                    got_wait(d, f, source)
        values = got[d, f].reshape(width, 2 * points)
        turned = jnp.concatenate([-values[:, points:], values[:, :points]], axis=1)
        real_rows = factor[f, :, 0].reshape(CORES * half_rows, width)
        imag_rows = factor[f, :, 1].reshape(CORES * half_rows, width)
        total = jnp.dot(real_rows, values, preferred_element_type=jnp.float32)
        total = total + jnp.dot(imag_rows, turned, preferred_element_type=jnp.float32)
        result[d, f] = total.astype(jnp.bfloat16).reshape(CORES, half_rows, 2 * points)
        output(d, f).start()
        (fwd_ref, adj_ref)[d][first + f] = result[d, f, side]

    for d, f in pairs:
        for a in (2 * d, 2 * d + 1):
            remote_load(a, f).wait_send()
        for step in range(1, group):
            near_copy(d, f, step).wait_send()
        if (d, f) in through:
            pack_copy(d, f).wait_send()

            @pl.when(is_gate)
            def _():
                for slot in range(CORES):
                    for step in range(1, group):
                        relay_copy(d, f, slot, step).wait_send()
        else:
            for step in range(group):
                far_copy(d, f, step).wait_send()
        output(d, f).wait()


def copy_out(*refs):
    srcs, dsts, sem = refs[:2], refs[2:4], refs[4]
    copies = [
        pltpu.make_async_copy(src.at[f], dst.at[f], sem.at[n, f])
        for n, (src, dst) in enumerate(zip(srcs, dsts)) for f in range(src.shape[0])
    ]
    for copy in copies:
        copy.start()
    for copy in copies:
        copy.wait()


def body(sources_field, residual_field, v_factors, u_factors, tile_class):
    freqs, _, half_rows, width = v_factors.shape
    tiles = tile_class.shape[1]
    points2 = sources_field.shape[2]
    own = freqs // CORES
    rank = width // tiles
    group = tiles // 2
    pack = packed_rows(tiles)
    any_spec = pl.BlockSpec(memory_space=pl.ANY)
    dma = pltpu.SemaphoreType.DMA
    bf16 = jnp.bfloat16
    out = jax.ShapeDtypeStruct(sources_field.shape, bf16)
    flops = 2 * 2 * 2 * freqs * 2 * half_rows * width * points2
    fields = pl.pallas_call(
        kernel,
        out_shape=(pltpu.VMEM(out.shape, bf16), pltpu.VMEM(out.shape, bf16)),
        in_specs=[pl.BlockSpec(memory_space=pltpu.SMEM)] + [pl.BlockSpec(memory_space=pltpu.HBM)] * 4,
        out_specs=(pl.BlockSpec(memory_space=pltpu.VMEM),) * 2,
        scratch_shapes=[
            pltpu.VMEM((own, CORES, 2, half_rows, width), bf16),
            pltpu.VMEM((own, CORES, 2, half_rows, width), bf16),
            pltpu.VMEM((own, CORES, half_rows, points2), bf16),
            pltpu.VMEM((own, CORES, half_rows, points2), bf16),
            pltpu.VMEM((2, own, tiles, rank, points2), bf16),
            pltpu.VMEM((2, own, pack, points2), bf16),
            pltpu.VMEM((2, own, CORES, pack, points2), bf16),
            pltpu.VMEM((2, own, CORES, group, rank, points2), bf16),
            pltpu.VMEM((2, own, tiles, rank, points2), bf16),
            pltpu.VMEM((2, own, CORES, half_rows, points2), bf16),
            dma((4, own)), dma((4, own)), dma((4, own)),
            dma((2, own, group)), dma((2, own, group)), dma((2, own, tiles)),
            dma((2, own)), dma((2, own, CORES)), dma((2, own, CORES, group)),
            dma((2, own)), dma((2, own)),
        ],
        compiler_params=pltpu.CompilerParams(
            collective_id=0, has_side_effects=True, vmem_limit_bytes=VMEM_LIMIT),
        cost_estimate=pl.CostEstimate(
            flops=flops, transcendentals=0, bytes_accessed=4 * v_factors.size + 8 * sources_field.size),
    )(tile_class, sources_field, residual_field, v_factors, u_factors)
    return pl.pallas_call(
        copy_out,
        out_shape=(out, out),
        in_specs=[pl.BlockSpec(memory_space=pltpu.VMEM)] * 2,
        out_specs=(any_spec, any_spec),
        scratch_shapes=[dma((2, freqs))],
        compiler_params=pltpu.CompilerParams(vmem_limit_bytes=4 * 1024 * 1024),
    )(*fields)


def solution(mesh):
    placed = (
        P("patch", "col", None),
        P("patch", "col", None),
        P("patch", None, "col", None),
        P("patch", None, "col", None),
        P("patch", None, None),
    )
    return jax.shard_map(
        body,
        mesh=mesh,
        in_specs=placed,
        out_specs=(P("patch", "col", None), P("patch", "col", None)),
        check_vma=False,
    )
```

```python
import jax
import jax.numpy as jnp
from jax import lax
from jax.experimental import pallas as pl
from jax.experimental.pallas import tpu as pltpu
from jax.sharding import PartitionSpec as P

RANKS = (8, 16, 32, 48)
CORES = 2
GROUP = 384
VMEM_LIMIT = 56 * 1024 * 1024
MESH = pl.DeviceIdType.MESH
THROUGH = 2


def packed_rows(tiles):
    return tiles // 8 * RANKS[3] + tiles // 4 * RANKS[2] + tiles // 8 * RANKS[1]


def kernel(
    class_ref, x_ref, r_ref, v_ref, u_ref, fwd_ref, adj_ref,
    v_all, u_all, x_all, r_all, coeff, packed, landed, relayed, got, result,
    in_sem, in_send, in_recv, near_send, far_send, got_recv, pack_send, pack_recv, relay_send,
    out_send, out_recv,
):
    freqs, _, half_rows, width = v_ref.shape
    tiles = class_ref.shape[1]
    rank = width // tiles
    points = x_ref.shape[2] // 2
    own = freqs // CORES
    index = lax.axis_index("col")
    tile = index // CORES
    side = index % CORES
    sibling = tile * CORES + 1 - side
    first = side * own
    other_first = (1 - side) * own
    group = tiles // 2
    inner = tiles // 4
    upper = tile // group
    place = tile % group
    near_base = upper * group
    far_base = (1 - upper) * group
    lane = place % inner
    gate = far_base + lane + upper * (group - inner)
    slot_out = place // inner
    is_gate = (place // inner) == (1 - upper)

    loads = ((v_ref, v_all), (x_ref, x_all), (u_ref, u_all), (r_ref, r_all))

    def local_load(a, f):
        src, dst = loads[a]
        return pltpu.make_async_copy(src.at[first + f], dst.at[f, side], in_sem.at[a, f])

    def remote_load(a, f):
        src, dst = loads[a]
        return pltpu.make_async_remote_copy(
            src_ref=src.at[other_first + f], dst_ref=dst.at[f, side],
            send_sem=in_send.at[a, f], recv_sem=in_recv.at[a, f],
            device_id={"col": sibling}, device_id_type=MESH,
        )

    pairs = [(d, f) for d in range(2) for f in range(own)]
    through = pairs[:THROUGH]
    barrier = pltpu.get_barrier_semaphore()
    pl.semaphore_signal(barrier, inc=1, device_id={"col": sibling}, device_id_type=MESH)
    for step in range(1, tiles):
        peer = ((tile + step) % tiles) * CORES + side
        pl.semaphore_signal(barrier, inc=1, device_id={"col": peer}, device_id_type=MESH)
    for d, f in pairs:
        local_load(2 * d, f).start()
        local_load(2 * d + 1, f).start()
    pl.semaphore_wait(barrier, tiles)

    for d, f in pairs:
        remote_load(2 * d, f).start()
        remote_load(2 * d + 1, f).start()

    def live(d, f, source, target):
        cls = class_ref[first + f, target, source] if d == 0 else class_ref[first + f, source, target]
        return jnp.where(cls == 0, RANKS[0], jnp.where(
            cls == 1, RANKS[1], jnp.where(cls == 2, RANKS[2], RANKS[3])))

    pack_rows = packed.shape[2]

    def selection(d, f, source, base):
        col = lax.broadcasted_iota(jnp.int32, (1, group * rank), 1)
        spot = jnp.full((1, group * rank), -1, jnp.int32)
        start = jnp.int32(0)
        for q in range(group):
            alive = live(d, f, source, base + q)
            inside = (col >= q * rank) & (col < q * rank + alive)
            spot = jnp.where(inside, col + (start - q * rank), spot)
            start = start + alive
        rows = lax.broadcasted_iota(jnp.int32, (pack_rows, group * rank), 0)
        return jnp.where(rows == spot, 1.0, 0.0).astype(jnp.bfloat16)

    def pack_copy(d, f):
        return pltpu.make_async_remote_copy(
            src_ref=packed.at[d, f], dst_ref=landed.at[d, f, slot_out],
            send_sem=pack_send.at[d, f], recv_sem=pack_recv.at[d, f, slot_out],
            device_id={"col": gate * CORES + side}, device_id_type=MESH)

    def pack_wait(d, f, slot):
        return pltpu.make_async_remote_copy(
            src_ref=packed.at[d, f], dst_ref=landed.at[d, f, slot],
            send_sem=pack_send.at[d, f], recv_sem=pack_recv.at[d, f, slot],
            device_id={"col": gate * CORES + side}, device_id_type=MESH)

    def near_copy(d, f, step):
        q = (place + step) % group
        return pltpu.make_async_remote_copy(
            src_ref=coeff.at[d, f, near_base + q], dst_ref=got.at[d, f, tile],
            send_sem=near_send.at[d, f, step], recv_sem=got_recv.at[d, f, tile],
            device_id={"col": (near_base + q) * CORES + side}, device_id_type=MESH)

    def relay_copy(d, f, slot, step):
        q = (place + step) % group
        source = far_base + slot * inner + lane
        return pltpu.make_async_remote_copy(
            src_ref=relayed.at[d, f, slot, q], dst_ref=got.at[d, f, source],
            send_sem=relay_send.at[d, f, slot, step], recv_sem=got_recv.at[d, f, source],
            device_id={"col": (near_base + q) * CORES + side}, device_id_type=MESH)

    def got_wait(d, f, source):
        pltpu.make_async_remote_copy(
            src_ref=coeff.at[d, f, source], dst_ref=got.at[d, f, source],
            send_sem=near_send.at[d, f, 0], recv_sem=got_recv.at[d, f, source],
            device_id={"col": sibling}, device_id_type=MESH).wait_recv()

    def far_copy(d, f, step):
        q = (place + step) % group
        return pltpu.make_async_remote_copy(
            src_ref=coeff.at[d, f, far_base + q], dst_ref=got.at[d, f, tile],
            send_sem=far_send.at[d, f, step], recv_sem=got_recv.at[d, f, tile],
            device_id={"col": (far_base + q) * CORES + side}, device_id_type=MESH)

    row = lax.broadcasted_iota(jnp.int32, (rank, 2 * points), 0)
    for d, f in pairs:
        factor, field = ((v_all, x_all), (u_all, r_all))[d]
        for a in (2 * d, 2 * d + 1):
            local_load(a, f).wait()
            remote_load(a, f).wait_recv()
        parts = []
        for half in range(CORES):
            block = field[f, half]
            parts += [block, jnp.concatenate([block[:, points:], -block[:, :points]], axis=1)]
        operand = jnp.concatenate(parts, axis=0)
        wide = GROUP if width % GROUP == 0 else width
        for g in range(width // wide):
            stacked = factor[f, :, :, :, g * wide:(g + 1) * wide]
            stacked = stacked.reshape(2 * CORES * half_rows, wide)
            sums = lax.dot_general(
                stacked, operand, (((0,), (0,)), ((), ())), preferred_element_type=jnp.float32)
            for k in range(wide // rank):
                to = g * (wide // rank) + k
                alive = live(d, f, tile, to)
                kept = jnp.where(row < alive, sums[k * rank:(k + 1) * rank], 0.0)
                coeff[d, f, to] = kept.astype(jnp.bfloat16)
        for step in range(1, group):
            near_copy(d, f, step).start()
        if (d, f) in through:
            far = coeff[d, f, pl.ds(far_base, group)].reshape(group * rank, 2 * points)
            packed[d, f] = jnp.dot(
                selection(d, f, tile, far_base), far,
                preferred_element_type=jnp.float32).astype(jnp.bfloat16)
            pack_copy(d, f).start()
        else:
            for step in range(group):
                far_copy(d, f, step).start()

    def relay(d, f):
        @pl.when(is_gate)
        def _():
            for slot in range(CORES):
                source = far_base + slot * inner + lane
                pack_wait(d, f, slot).wait_recv()
                full = lax.dot_general(
                    selection(d, f, source, near_base), landed[d, f, slot],
                    (((0,), (0,)), ((), ())), preferred_element_type=jnp.float32)
                relayed[d, f, slot] = full.astype(jnp.bfloat16).reshape(group, rank, 2 * points)
                for step in range(1, group):
                    relay_copy(d, f, slot, step).start()
                got[d, f, source] = relayed[d, f, slot, place]

    def output(d, f):
        return pltpu.make_async_remote_copy(
            src_ref=result.at[d, f, 1 - side], dst_ref=(fwd_ref, adj_ref)[d].at[first + f],
            send_sem=out_send.at[d, f], recv_sem=out_recv.at[d, f],
            device_id={"col": sibling}, device_id_type=MESH,
        )

    for d, f in through:
        relay(d, f)

    for d, f in pairs:
        factor = (u_all, v_all)[d]
        got[d, f, tile] = coeff[d, f, tile]
        for step in range(1, group):
            got_wait(d, f, near_base + (place + step) % group)
        for slot in range(CORES):
            for at in range(inner):
                source = far_base + slot * inner + at
                if (d, f) not in through:
                    got_wait(d, f, source)
                    continue

                @pl.when(jnp.logical_not(is_gate & (lane == at)))
                def _():
                    got_wait(d, f, source)
        values = got[d, f].reshape(width, 2 * points)
        turned = jnp.concatenate([-values[:, points:], values[:, :points]], axis=1)
        real_rows = factor[f, :, 0].reshape(CORES * half_rows, width)
        imag_rows = factor[f, :, 1].reshape(CORES * half_rows, width)
        total = jnp.dot(real_rows, values, preferred_element_type=jnp.float32)
        total = total + jnp.dot(imag_rows, turned, preferred_element_type=jnp.float32)
        result[d, f] = total.astype(jnp.bfloat16).reshape(CORES, half_rows, 2 * points)
        output(d, f).start()
        (fwd_ref, adj_ref)[d][first + f] = result[d, f, side]

    for d, f in pairs:
        for a in (2 * d, 2 * d + 1):
            remote_load(a, f).wait_send()
        for step in range(1, group):
            near_copy(d, f, step).wait_send()
        if (d, f) in through:
            pack_copy(d, f).wait_send()

            @pl.when(is_gate)
            def _():
                for slot in range(CORES):
                    for step in range(1, group):
                        relay_copy(d, f, slot, step).wait_send()
        else:
            for step in range(group):
                far_copy(d, f, step).wait_send()
        output(d, f).wait()


def copy_out(*refs):
    srcs, dsts, sem = refs[:2], refs[2:4], refs[4]
    copies = [
        pltpu.make_async_copy(src.at[f], dst.at[f], sem.at[n, f])
        for n, (src, dst) in enumerate(zip(srcs, dsts)) for f in range(src.shape[0])
    ]
    for copy in copies:
        copy.start()
    for copy in copies:
        copy.wait()


def body(sources_field, residual_field, v_factors, u_factors, tile_class):
    freqs, _, half_rows, width = v_factors.shape
    tiles = tile_class.shape[1]
    points2 = sources_field.shape[2]
    own = freqs // CORES
    rank = width // tiles
    group = tiles // 2
    pack = packed_rows(tiles)
    any_spec = pl.BlockSpec(memory_space=pl.ANY)
    dma = pltpu.SemaphoreType.DMA
    bf16 = jnp.bfloat16
    out = jax.ShapeDtypeStruct(sources_field.shape, bf16)
    flops = 2 * 2 * 2 * freqs * 2 * half_rows * width * points2
    fields = pl.pallas_call(
        kernel,
        out_shape=(pltpu.VMEM(out.shape, bf16), pltpu.VMEM(out.shape, bf16)),
        in_specs=[pl.BlockSpec(memory_space=pltpu.SMEM)] + [pl.BlockSpec(memory_space=pltpu.HBM)] * 4,
        out_specs=(pl.BlockSpec(memory_space=pltpu.VMEM),) * 2,
        scratch_shapes=[
            pltpu.VMEM((own, CORES, 2, half_rows, width), bf16),
            pltpu.VMEM((own, CORES, 2, half_rows, width), bf16),
            pltpu.VMEM((own, CORES, half_rows, points2), bf16),
            pltpu.VMEM((own, CORES, half_rows, points2), bf16),
            pltpu.VMEM((2, own, tiles, rank, points2), bf16),
            pltpu.VMEM((2, own, pack, points2), bf16),
            pltpu.VMEM((2, own, CORES, pack, points2), bf16),
            pltpu.VMEM((2, own, CORES, group, rank, points2), bf16),
            pltpu.VMEM((2, own, tiles, rank, points2), bf16),
            pltpu.VMEM((2, own, CORES, half_rows, points2), bf16),
            dma((4, own)), dma((4, own)), dma((4, own)),
            dma((2, own, group)), dma((2, own, group)), dma((2, own, tiles)),
            dma((2, own)), dma((2, own, CORES)), dma((2, own, CORES, group)),
            dma((2, own)), dma((2, own)),
        ],
        compiler_params=pltpu.CompilerParams(
            collective_id=0, has_side_effects=True, vmem_limit_bytes=VMEM_LIMIT),
        cost_estimate=pl.CostEstimate(
            flops=flops, transcendentals=0, bytes_accessed=4 * v_factors.size + 8 * sources_field.size),
    )(tile_class, sources_field, residual_field, v_factors, u_factors)
    return pl.pallas_call(
        copy_out,
        out_shape=(out, out),
        in_specs=[pl.BlockSpec(memory_space=pltpu.VMEM)] * 2,
        out_specs=(any_spec, any_spec),
        scratch_shapes=[dma((2, freqs))],
        compiler_params=pltpu.CompilerParams(vmem_limit_bytes=4 * 1024 * 1024),
    )(*fields)


def solution(mesh):
    placed = (
        P("patch", "col", None),
        P("patch", "col", None),
        P("patch", None, "col", None),
        P("patch", None, "col", None),
        P("patch", None, None),
    )
    return jax.shard_map(
        body,
        mesh=mesh,
        in_specs=placed,
        out_specs=(P("patch", "col", None), P("patch", "col", None)),
        check_vma=False,
    )
```
